256 devices in a mesh: span: 4 (over x), seq: 32 (over z, y), tp: 2 (over core).
Axes of the slice: x: 4, y: 4, z: 8, core: 2. Of those that a mesh axis runs over, the one named last changes fastest.
Arguments:
- query_states: bfloat16 [4, 3072, 4096], P('span', ('seq', 'tp')), may hold values from -8 to 8
- key_states: bfloat16 [4, 3072, 4096], P('span', ('seq', 'tp')), may hold values from -8 to 8
- value_states: bfloat16 [4, 3072, 4096], P('span', ('seq', 'tp')), may hold values from -6 to 6
- frame_mask: int32 [4, 96], replicated, may hold values from 0 to 1, as said below
- levels: int32 [4], P('span'), may hold values from 0 to 15
- gate_table: float32 [16, 4096], replicated, may hold values from 0.1 to 1.9
Outputs:
- gated_out: bfloat16 [4, 3072, 4096], P('span', ('seq', 'tp'))
The draws below stay inside these ranges and needn't reach their ends.
Inputs may be any that keep to these rules, and one draw needn't show every extreme that they name: frame_mask[c, f] is 1 for every frame f of span c and 0 for every frame of later spans.
All inputs are finite; a program needn't handle non-finite values.
Results may differ from the reference program's by a relative error of at most 0.006.
Values may be sent and summed in bfloat16 or wider, within the bound.
A program may use at most 128 MiB of HBM per device.

```python
import math
import jax
import jax.numpy as jnp
from jax import lax

HEAD = 128
FRAMES = 24
LEVELS = 16
HEADS = 32
SPANS = 4
CTOK = 3072
TPF = 128


def draw_query_states(key, part):
    key = jax.random.fold_in(key, 2)
    shape = (SPANS, CTOK, HEADS * HEAD)
    drawn = jnp.clip(2.8 * jax.random.normal(key, shape, jnp.float32), -8.0, 8.0)
    return drawn.astype(jnp.bfloat16)


def draw_key_states(key, part):
    key = jax.random.fold_in(key, 3)
    shape = (SPANS, CTOK, HEADS * HEAD)
    drawn = jnp.clip(jax.random.normal(key, shape, jnp.float32), -6.0, 6.0)
    return drawn.astype(jnp.bfloat16)


def draw_frame_mask(key, part):
    key = jax.random.fold_in(key, 5)
    owner = jnp.arange(SPANS * FRAMES, dtype=jnp.int32) // FRAMES
    reader = jnp.arange(SPANS, dtype=jnp.int32)[:, None]
    coin = jax.random.randint(key, (SPANS, SPANS * FRAMES), 0, 2).astype(jnp.int32)
    own = owner[None, :] == reader
    older = owner[None, :] < reader
    return jnp.where(own, 1, jnp.where(older, coin, 0)).astype(jnp.int32)


def plant(entries, stream_key, least, high):
    place = [jax.random.randint(jax.random.fold_in(stream_key, axis), (), 0, length) for axis, length in enumerate(entries.shape)]
    longest = entries.shape.index(max(entries.shape))
    beside = place[:longest] + [(place[longest] + 1) % entries.shape[longest]] + place[longest + 1:]
    return entries.at[tuple(place)].set(least).at[tuple(beside)].set(high)


def level_of(key, shape, cuts, low, largest):
    def one(axis_at, blocks):
        draws = jax.random.uniform(jax.random.fold_in(jax.random.fold_in(key, 6), axis_at), (blocks,), jnp.float32, low / len(cuts), largest / len(cuts))
        return jnp.repeat(jnp.exp(draws), shape[axis_at] // blocks).reshape((-1,) + (1,) * (len(shape) - axis_at - 1))

    level = one(*cuts[0])
    for cut in cuts[1:]:
        level = level * one(*cut)
    return level


def normal_values(stream_key, dims, spread, reach, pieces=(), held_as=jnp.bfloat16):
    result = jax.random.normal(stream_key, dims, jnp.float32) * spread
    if len(pieces) > 0:
        result = level_of(stream_key, dims, pieces, -0.22, 0.18) * result
    return jnp.clip(result, min=-reach, max=reach).astype(held_as)


def setup_inputs(seed: int = 0) -> dict:
    arg_keys = jax.random.split(jax.random.key(seed), 7)
    query_states = draw_query_states(jax.random.fold_in(arg_keys[6], 71), 0)
    key_states = draw_key_states(jax.random.fold_in(arg_keys[6], 71), 0)
    value_states = normal_values(arg_keys[2], (SPANS, CTOK, HEADS * HEAD), 1.0, 6.0, ((0, 4), (1, 64)))
    frame_mask = draw_frame_mask(jax.random.fold_in(arg_keys[6], 71), 0)
    levels = plant(jax.random.randint(arg_keys[4], (SPANS,), 0, LEVELS), jax.random.fold_in(arg_keys[4], 1), 0, LEVELS - 1).astype(jnp.int32)
    gate_table = jnp.clip(1.0 + 0.18 * jax.random.normal(arg_keys[5], (LEVELS, HEADS * HEAD), jnp.float32), 0.1, 1.9)
    return dict(query_states=query_states, key_states=key_states, value_states=value_states, frame_mask=frame_mask, levels=levels, gate_table=gate_table)


def reference(query_states, key_states, value_states, frame_mask, levels, gate_table):
    scale = 1.0 / math.sqrt(HEAD)
    visible_all = jnp.repeat(frame_mask, TPF, axis=1) > 0
    query_heads = query_states.reshape(SPANS, CTOK, HEADS, HEAD).transpose(2, 0, 1, 3)
    key_heads = key_states.reshape(SPANS * CTOK, HEADS, HEAD).transpose(1, 0, 2)
    value_heads = value_states.reshape(SPANS * CTOK, HEADS, HEAD).transpose(1, 0, 2)

    def one_head(operands):
        query_head, key_head, value_head = operands
        outputs = []
        for span in range(SPANS):
            visible = visible_all[span]
            scores = jnp.dot(query_head[span], key_head.T, preferred_element_type=jnp.float32) * scale
            scores = jnp.where(visible[None, :], scores, -1e+30)
            row_max = lax.optimization_barrier(jnp.max(scores, axis=1))
            weights = jnp.where(visible[None, :], jnp.exp(scores - row_max[:, None]), 0.0)
            rounded = weights.astype(jnp.bfloat16)
            summed = jnp.dot(rounded, value_head, preferred_element_type=jnp.float32)
            outputs.append(summed / lax.optimization_barrier(jnp.sum(weights, axis=1))[:, None])
        return jnp.stack(outputs)
    attended = lax.map(one_head, (query_heads, key_heads, value_heads))
    attended = attended.transpose(1, 2, 0, 3).reshape(SPANS, CTOK, HEADS * HEAD).astype(jnp.bfloat16)
    gate_rows = gate_table[levels]
    return (gate_rows[:, None, :] * attended.astype(jnp.float32)).astype(jnp.bfloat16)
```

```python
import functools
import math

import jax
import jax.numpy as jnp
from jax import lax
from jax.experimental import pallas as pl
from jax.experimental.pallas import tpu as pltpu
from jax.sharding import PartitionSpec as P

MESH = pl.DeviceIdType.MESH
HEAD = 128
SPANS = 4
NX, NY, NZ = 4, 4, 8
ROWS = 48
FRAMES = 24
QROWS = NZ * ROWS
FEATURES = NX * NZ * HEAD
LOG2_SCALE = math.log2(math.e) / math.sqrt(HEAD)
NEG = -1e30
K, V, Q = 0, 1, 2


def body(
    levels, mask, q_in, k_in, v_in, gate, out,
    kbuf, vbuf, qbuf, sbuf, mine, merged,
    a2a_send, a2a_recv, y_send, y_recv, c_send, c_recv, o_send, o_recv,
):
    x = lax.axis_index("span")
    s = lax.axis_index("seq")
    c = lax.axis_index("tp")
    y, z = s % NY, s // NY
    up, down, far = (y + 1) % NY, (y + NY - 1) % NY, (y + 2) % NY
    head = x * NZ + z

    def peer(i):
        return (x + i // NZ) % NX, (z + i % NZ) % NZ

    barrier = pltpu.get_barrier_semaphore()

    def greet(i, carry):
        px, pz = peer(i)
        pl.semaphore_signal(barrier, inc=1, device_id=(px, pz * NY + y, c), device_id_type=MESH)
        return carry

    lax.fori_loop(1, NX * NZ, greet, 0)
    for to in ((x, z * NY + up, c), (x, z * NY + down, c), (x, s, 1 - c)):
        pl.semaphore_signal(barrier, inc=1, device_id=to, device_id_type=MESH)

    for span in range(SPANS):
        vbuf[span, :, :, :, HEAD:] = jnp.ones((NZ, NY * 2, ROWS, HEAD), jnp.bfloat16)

    pl.semaphore_wait(barrier, NX * NZ - 1 + 3)

    def cols(h):
        return pl.ds(pl.multiple_of(h * HEAD, HEAD), HEAD)

    srcs = (k_in, v_in, q_in)

    def block(arr, span, zs, who):
        if arr == Q:
            return qbuf.at[span, zs]
        if arr == K:
            return kbuf.at[span, zs, who]
        return vbuf.at[span, zs, who, :, pl.ds(0, HEAD)]

    whole, low, high = pl.ds(0, NZ), pl.ds(0, NZ // 2), pl.ds(NZ // 2, NZ // 2)
    me = y * 2 + c
    lo, hi, across = down * 2 + c, up * 2 + c, far * 2 + c

    def issue(arr):
        pltpu.make_async_copy(srcs[arr].at[:, cols(head)], block(arr, x, z, me), a2a_recv.at[arr, x]).start()

        def one(i, carry):
            px, pz = peer(i)
            pltpu.make_async_remote_copy(
                src_ref=srcs[arr].at[:, cols(px * NZ + pz)],
                dst_ref=block(arr, x, z, me),
                send_sem=a2a_send.at[arr],
                recv_sem=a2a_recv.at[arr, x],
                device_id=(px, pz * NY + y, c),
                device_id_type=MESH,
            ).start()
            return carry

        lax.fori_loop(1, NX * NZ, one, 0)

    def arrived(arr, span):
        b = block(arr, span, whole, me)
        pltpu.make_async_copy(b, b, a2a_recv.at[arr, span]).wait()

    def y_copy(arr, span, zs, who, to, kind):
        b = block(arr, span, zs, who)
        return pltpu.make_async_remote_copy(
            src_ref=b, dst_ref=b, send_sem=y_send.at[arr, span, kind], recv_sem=y_recv.at[arr, span, kind],
            device_id=(x, z * NY + to, c), device_id_type=MESH)

    def c_copy(arr, span, zs, who, kind):
        b = block(arr, span, zs, who)
        return pltpu.make_async_remote_copy(
            src_ref=b, dst_ref=b, send_sem=c_send.at[arr, span, kind], recv_sem=c_recv.at[arr, span, kind],
            device_id=(x, s, 1 - c), device_id_type=MESH)

    def share(arr, span):
        arrived(arr, span)
        y_copy(arr, span, whole, me, up, 0).start()
        y_copy(arr, span, whole, me, down, 1).start()
        c_copy(arr, span, whole, me, 0).start()

    def forward(arr, span):
        y_copy(arr, span, whole, lo, up, 0).wait_recv()
        y_copy(arr, span, low, lo, up, 2).start()
        c_copy(arr, span, whole, lo, 1).start()
        y_copy(arr, span, whole, hi, down, 1).wait_recv()
        y_copy(arr, span, high, hi, down, 3).start()
        c_copy(arr, span, whole, hi, 2).start()

    def finish(arr, span):
        y_copy(arr, span, low, across, up, 2).wait_recv()
        c_copy(arr, span, low, across, 3).start()
        y_copy(arr, span, high, across, down, 3).wait_recv()
        c_copy(arr, span, high, across, 4).start()

    def collect(arr, span):
        for kind, zs in enumerate((whole, whole, whole, low, high)):
            c_copy(arr, span, zs, me, kind).wait_recv()

    issue(K)
    issue(V)
    todo = [(arr, (x + NX - i) % NX) for arr in (K, V) for i in range(NX)]
    for n in range(len(todo) + 3):
        if n == 3:
            issue(Q)
        if n < len(todo):
            share(*todo[n])
        if 0 <= n - 1 < len(todo):
            forward(*todo[n - 1])
        if 0 <= n - 2 < len(todo):
            finish(*todo[n - 2])
        if 0 <= n - 3 < len(todo):
            collect(*todo[n - 3])

    def score(own, span, mx, masked):
        keys = kbuf[span].reshape(FRAMES * HEAD, HEAD)
        sc = lax.dot_general(
            qbuf[own].reshape(QROWS, HEAD), keys, (((1,), (1,)), ((), ())), preferred_element_type=jnp.float32)
        for f in range(FRAMES):
            part = sc[:, f * HEAD : (f + 1) * HEAD]
            if masked:
                part = part + jnp.where(mask[own, span * FRAMES + f] > 0, 0.0, NEG).astype(jnp.float32)
            sbuf[span * FRAMES + f] = part
            mx = jnp.maximum(mx, part)
        return mx

    def weigh(span, top, total):
        parts = [
            jnp.exp2(sbuf[span * FRAMES + f] * LOG2_SCALE - top).astype(jnp.bfloat16) for f in range(FRAMES)
        ]
        values = vbuf[span].reshape(FRAMES * HEAD, 2 * HEAD)
        return total + jnp.dot(jnp.concatenate(parts, axis=1), values, preferred_element_type=jnp.float32)

    def give(own, dz):
        pz = (z + dz) % NZ
        return pltpu.make_async_remote_copy(
            src_ref=mine.at[own, pz], dst_ref=merged.at[:, cols(head)], send_sem=o_send, recv_sem=o_recv,
            device_id=(own, pz * NY + y, c), device_id_type=MESH)

    for own in range(SPANS):
        arrived(Q, own)
        mx = jnp.full((QROWS, HEAD), NEG, jnp.float32)
        mx = score(own, own, mx, False)
        if own:
            mx = lax.fori_loop(0, own, lambda i, cur: score(own, i, cur, True), mx)
        top = jnp.broadcast_to(jnp.max(mx, axis=1, keepdims=True) * LOG2_SCALE, (QROWS, HEAD))
        total = lax.fori_loop(
            0, own + 1, lambda i, cur: weigh(i, top, cur), jnp.zeros((QROWS, 2 * HEAD), jnp.float32))
        result = (total[:, :HEAD] / total[:, HEAD:]).astype(jnp.bfloat16)
        mine[own] = result.reshape(NZ, ROWS, HEAD)
        for dz in range(1, NZ):
            give(own, dz).start()

        @pl.when(x != own)
        def _():
            give(own, 0).start()

        @pl.when(x == own)
        def _():
            pltpu.make_async_copy(mine.at[own, z], merged.at[:, cols(head)], o_recv).start()

    row = gate[pl.ds(levels[0], 1), :]
    pltpu.make_async_copy(merged, merged, o_recv).wait()
    out[...] = (row * merged[...].astype(jnp.float32)).astype(jnp.bfloat16)

    part = merged.at[:, pl.ds(0, FEATURES - HEAD)]
    pltpu.make_async_copy(part, part, o_send).wait()
    for arr in (K, V, Q):
        part = srcs[arr].at[:, pl.ds(0, FEATURES - HEAD)]
        pltpu.make_async_copy(part, part, a2a_send.at[arr]).wait()
    for arr, span in todo:
        for kind, zs in enumerate((whole, whole, low, high)):
            y_copy(arr, span, zs, me, up, kind).wait_send()
        for kind, zs in enumerate((whole, whole, whole, low, high)):
            c_copy(arr, span, zs, me, kind).wait_send()


def on_device(query_states, key_states, value_states, frame_mask, levels, gate_table):
    bf16 = jnp.bfloat16
    hbm = pl.BlockSpec(memory_space=pl.ANY)
    smem = pl.BlockSpec(memory_space=pltpu.SMEM)
    vmem = pl.BlockSpec(memory_space=pltpu.VMEM)
    dma = pltpu.SemaphoreType.DMA
    result = pl.pallas_call(
        body,
        out_shape=jax.ShapeDtypeStruct((ROWS, FEATURES), bf16),
        in_specs=[smem, smem, hbm, hbm, hbm, vmem],
        out_specs=vmem,
        scratch_shapes=[
            pltpu.VMEM((SPANS, NZ, NY * 2, ROWS, HEAD), bf16),
            pltpu.VMEM((SPANS, NZ, NY * 2, ROWS, 2 * HEAD), bf16),
            pltpu.VMEM((SPANS, NZ, ROWS, HEAD), bf16),
            pltpu.VMEM((SPANS * FRAMES, QROWS, HEAD), jnp.float32),
            pltpu.VMEM((SPANS, NZ, ROWS, HEAD), bf16),
            pltpu.VMEM((ROWS, FEATURES), bf16),
            dma((3,)),
            dma((3, SPANS)),
            dma((2, SPANS, 4)),
            dma((2, SPANS, 4)),
            dma((2, SPANS, 5)),
            dma((2, SPANS, 5)),
            dma,
            dma,
        ],
        compiler_params=pltpu.CompilerParams(
            collective_id=0, has_side_effects=True, vmem_limit_bytes=56 * 2**20
        ),
    )(levels, frame_mask, query_states[0], key_states[0], value_states[0], gate_table)
    return result[None]


def solution(mesh):
    split = P("span", ("seq", "tp"), None)
    return jax.shard_map(
        on_device,
        mesh=mesh,
        in_specs=(split, split, split, P(), P("span"), P()),
        out_specs=split,
        check_vma=False,
    )
```

```python
import functools
import math

import jax
import jax.numpy as jnp
from jax import lax
from jax.experimental import pallas as pl
from jax.experimental.pallas import tpu as pltpu
from jax.sharding import PartitionSpec as P

MESH = pl.DeviceIdType.MESH
HEAD = 128
SPANS = 4
NX, NY, NZ = 4, 4, 8
ROWS = 48
FRAMES = 24
QROWS = NZ * ROWS
FEATURES = NX * NZ * HEAD
LOG2_SCALE = math.log2(math.e) / math.sqrt(HEAD)
NEG = -1e30
K, V, Q = 0, 1, 2


def body(
    levels, mask, q_in, k_in, v_in, gate, out,
    kbuf, vbuf, qbuf, sbuf, peak, mine, merged,
    a2a_send, a2a_recv, y_send, y_recv, c_send, c_recv, o_send, o_recv,
):
    x = lax.axis_index("span")
    s = lax.axis_index("seq")
    c = lax.axis_index("tp")
    y, z = s % NY, s // NY
    up, down, far = (y + 1) % NY, (y + NY - 1) % NY, (y + 2) % NY
    head = x * NZ + z

    def peer(i):
        return (x + i // NZ) % NX, (z + i % NZ) % NZ

    barrier = pltpu.get_barrier_semaphore()

    def greet(i, carry):
        px, pz = peer(i)
        pl.semaphore_signal(barrier, inc=1, device_id=(px, pz * NY + y, c), device_id_type=MESH)
        return carry

    lax.fori_loop(1, NX * NZ, greet, 0)
    for to in ((x, z * NY + up, c), (x, z * NY + down, c), (x, s, 1 - c)):
        pl.semaphore_signal(barrier, inc=1, device_id=to, device_id_type=MESH)

    for span in range(SPANS):
        vbuf[span, :, :, :, HEAD:] = jnp.ones((NZ, NY * 2, ROWS, HEAD), jnp.bfloat16)

    pl.semaphore_wait(barrier, NX * NZ - 1 + 3)

    def cols(h):
        return pl.ds(pl.multiple_of(h * HEAD, HEAD), HEAD)

    srcs = (k_in, v_in, q_in)

    def block(arr, span, zs, who):
        if arr == Q:
            return qbuf.at[span, zs]
        if arr == K:
            return kbuf.at[span, zs, who]
        return vbuf.at[span, zs, who, :, pl.ds(0, HEAD)]

    whole, low, high = pl.ds(0, NZ), pl.ds(0, NZ // 2), pl.ds(NZ // 2, NZ // 2)
    me = y * 2 + c
    lo, hi, across = down * 2 + c, up * 2 + c, far * 2 + c

    def issue(arr, start=0, stop=NX):
        if start == 0:
            pltpu.make_async_copy(srcs[arr].at[:, cols(head)], block(arr, x, z, me), a2a_recv.at[arr, x]).start()

        def one(i, carry):
            px, pz = peer(i)
            pltpu.make_async_remote_copy(
                src_ref=srcs[arr].at[:, cols(px * NZ + pz)],
                dst_ref=block(arr, x, z, me),
                send_sem=a2a_send.at[arr],
                recv_sem=a2a_recv.at[arr, x],
                device_id=(px, pz * NY + y, c),
                device_id_type=MESH,
            ).start()
            return carry

        lax.fori_loop(max(1, start * NZ), stop * NZ, one, 0)

    def arrived(arr, span):
        b = block(arr, span, whole, me)
        pltpu.make_async_copy(b, b, a2a_recv.at[arr, span]).wait()

    def y_copy(arr, span, zs, who, to, kind):
        b = block(arr, span, zs, who)
        return pltpu.make_async_remote_copy(
            src_ref=b, dst_ref=b, send_sem=y_send.at[arr, span, kind], recv_sem=y_recv.at[arr, span, kind],
            device_id=(x, z * NY + to, c), device_id_type=MESH)

    def c_copy(arr, span, zs, who, kind):
        b = block(arr, span, zs, who)
        return pltpu.make_async_remote_copy(
            src_ref=b, dst_ref=b, send_sem=c_send.at[arr, span, kind], recv_sem=c_recv.at[arr, span, kind],
            device_id=(x, s, 1 - c), device_id_type=MESH)

    def share(arr, span):
        arrived(arr, span)
        y_copy(arr, span, whole, me, up, 0).start()
        y_copy(arr, span, whole, me, down, 1).start()
        c_copy(arr, span, whole, me, 0).start()

    def forward(arr, span):
        y_copy(arr, span, whole, lo, up, 0).wait_recv()
        y_copy(arr, span, low, lo, up, 2).start()
        c_copy(arr, span, whole, lo, 1).start()
        y_copy(arr, span, whole, hi, down, 1).wait_recv()
        y_copy(arr, span, high, hi, down, 3).start()
        c_copy(arr, span, whole, hi, 2).start()

    def finish(arr, span):
        y_copy(arr, span, low, across, up, 2).wait_recv()
        c_copy(arr, span, low, across, 3).start()
        y_copy(arr, span, high, across, down, 3).wait_recv()
        c_copy(arr, span, high, across, 4).start()

    def collect(arr, span):
        for kind, zs in enumerate((whole, whole, whole, low, high)):
            c_copy(arr, span, zs, me, kind).wait_recv()

    def unit(own, span):
        return (own * (own + 1) // 2 + span) * FRAMES

    def score(own, span, masked):
        keys = kbuf[span].reshape(FRAMES * HEAD, HEAD)
        sc = lax.dot_general(
            qbuf[own].reshape(QROWS, HEAD), keys, (((1,), (1,)), ((), ())), preferred_element_type=jnp.float32)
        mx = None if span is own else peak[own]
        for f in range(FRAMES):
            part = sc[:, f * HEAD : (f + 1) * HEAD]
            if masked:
                part = part + jnp.where(mask[own, span * FRAMES + f] > 0, 0.0, NEG).astype(jnp.float32)
            sbuf[unit(own, span) + f] = part
            mx = part if mx is None else jnp.maximum(mx, part)
        peak[own] = mx

    def weigh(own, span, top, total):
        parts = [
            jnp.exp2(sbuf[unit(own, span) + f] * LOG2_SCALE - top).astype(jnp.bfloat16) for f in range(FRAMES)
        ]
        values = vbuf[span].reshape(FRAMES * HEAD, 2 * HEAD)
        return total + jnp.dot(jnp.concatenate(parts, axis=1), values, preferred_element_type=jnp.float32)

    def give(own, dz):
        pz = (z + dz) % NZ
        return pltpu.make_async_remote_copy(
            src_ref=mine.at[own, pz], dst_ref=merged.at[:, cols(head)], send_sem=o_send, recv_sem=o_recv,
            device_id=(own, pz * NY + y, c), device_id_type=MESH)

    def olders(own, start, stop):
        lax.fori_loop(start, stop, lambda i, cur: score(own, i, True) or cur, 0)

    issue(K)
    issue(V)
    issue(Q)

    k0, k1, k2, k3 = [(x + NX - i) % NX for i in range(NX)]
    share(K, k0)
    share(K, k1)
    forward(K, k0)
    share(K, k2)
    forward(K, k1)
    share(K, k3)
    forward(K, k2)
    finish(K, k0)
    forward(K, k3)
    share(V, 0)
    finish(K, k1)
    finish(K, k2)
    share(V, 1)
    finish(K, k3)
    share(V, 2)
    share(V, 3)
    for span in range(SPANS):
        collect(K, span)
    forward(V, 0)

    def outputs(own, last=None):
        top = jnp.broadcast_to(jnp.max(peak[own], axis=1, keepdims=True) * LOG2_SCALE, (QROWS, HEAD))
        total = jnp.zeros((QROWS, 2 * HEAD), jnp.float32)
        if last is None:
            total = lax.fori_loop(0, own + 1, lambda i, cur: weigh(own, i, top, cur), total)
        else:
            total = lax.fori_loop(0, own, lambda i, cur: weigh(own, i, top, cur), total)
            last()
            total = weigh(own, own, top, total)
        result = (total[:, :HEAD] / total[:, HEAD:]).astype(jnp.bfloat16)
        mine[own] = result.reshape(NZ, ROWS, HEAD)
        for dz in range(1, NZ):
            give(own, dz).start()

        @pl.when(x != own)
        def _():
            give(own, 0).start()

        @pl.when(x == own)
        def _():
            pltpu.make_async_copy(mine.at[own, z], merged.at[:, cols(head)], o_recv).start()

    for own in range(SPANS):
        arrived(Q, own)
    score(0, 0, False)
    forward(V, 1)
    score(1, 1, False)
    finish(V, 0)
    forward(V, 2)
    olders(1, 0, 1)
    collect(V, 0)
    outputs(0)
    finish(V, 1)
    forward(V, 3)
    score(2, 2, False)
    collect(V, 1)
    outputs(1)
    finish(V, 2)
    olders(2, 0, 1)
    finish(V, 3)
    olders(2, 1, 2)
    collect(V, 2)
    outputs(2)
    score(3, 3, False)
    olders(3, 0, 3)
    outputs(3, lambda: collect(V, 3))

    row = gate[pl.ds(levels[0], 1), :]
    pltpu.make_async_copy(merged, merged, o_recv).wait()
    out[...] = (row * merged[...].astype(jnp.float32)).astype(jnp.bfloat16)

    part = merged.at[:, pl.ds(0, FEATURES - HEAD)]
    pltpu.make_async_copy(part, part, o_send).wait()
    for arr in (K, V, Q):
        part = srcs[arr].at[:, pl.ds(0, FEATURES - HEAD)]
        pltpu.make_async_copy(part, part, a2a_send.at[arr]).wait()
    for arr, span in [(arr, span) for arr in (K, V) for span in range(SPANS)]:
        for kind, zs in enumerate((whole, whole, low, high)):
            y_copy(arr, span, zs, me, up, kind).wait_send()
        for kind, zs in enumerate((whole, whole, whole, low, high)):
            c_copy(arr, span, zs, me, kind).wait_send()


def on_device(query_states, key_states, value_states, frame_mask, levels, gate_table):
    bf16 = jnp.bfloat16
    hbm = pl.BlockSpec(memory_space=pl.ANY)
    smem = pl.BlockSpec(memory_space=pltpu.SMEM)
    vmem = pl.BlockSpec(memory_space=pltpu.VMEM)
    dma = pltpu.SemaphoreType.DMA
    result = pl.pallas_call(
        body,
        out_shape=jax.ShapeDtypeStruct((ROWS, FEATURES), bf16),
        in_specs=[smem, smem, hbm, hbm, hbm, vmem],
        out_specs=vmem,
        scratch_shapes=[
            pltpu.VMEM((SPANS, NZ, NY * 2, ROWS, HEAD), bf16),
            pltpu.VMEM((SPANS, NZ, NY * 2, ROWS, 2 * HEAD), bf16),
            pltpu.VMEM((SPANS, NZ, ROWS, HEAD), bf16),
            pltpu.VMEM((10 * FRAMES, QROWS, HEAD), jnp.float32),
            pltpu.VMEM((SPANS, QROWS, HEAD), jnp.float32),
            pltpu.VMEM((SPANS, NZ, ROWS, HEAD), bf16),
            pltpu.VMEM((ROWS, FEATURES), bf16),
            dma((3,)),
            dma((3, SPANS)),
            dma((2, SPANS, 4)),
            dma((2, SPANS, 4)),
            dma((2, SPANS, 5)),
            dma((2, SPANS, 5)),
            dma,
            dma,
        ],
        compiler_params=pltpu.CompilerParams(
            collective_id=0, has_side_effects=True, vmem_limit_bytes=63 * 2**20
        ),
    )(levels, frame_mask, query_states[0], key_states[0], value_states[0], gate_table)
    return result[None]


def solution(mesh):
    split = P("span", ("seq", "tp"), None)
    return jax.shard_map(
        on_device,
        mesh=mesh,
        in_specs=(split, split, split, P(), P("span"), P()),
        out_specs=split,
        check_vma=False,
    )
```

```python
import functools
import math

import jax
import jax.numpy as jnp
from jax import lax
from jax.experimental import pallas as pl
from jax.experimental.pallas import tpu as pltpu
from jax.sharding import PartitionSpec as P

MESH = pl.DeviceIdType.MESH
HEAD = 128
SPANS = 4
NX, NY, NZ = 4, 4, 8
ROWS = 48
FRAMES = 24
QROWS = NZ * ROWS
FEATURES = NX * NZ * HEAD
LOG2_SCALE = math.log2(math.e) / math.sqrt(HEAD)
NEG = -1e30
K, V, Q = 0, 1, 2


def body(
    mask, q_in, k_in, v_in, merged,
    kbuf, vbuf, qbuf, sbuf, peak, mine,
    a2a_send, a2a_recv, y_send, y_recv, c_send, c_recv, o_send, o_recv,
):
    x = lax.axis_index("span")
    s = lax.axis_index("seq")
    c = lax.axis_index("tp")
    y, z = s % NY, s // NY
    up, down, far = (y + 1) % NY, (y + NY - 1) % NY, (y + 2) % NY
    head = x * NZ + z

    def peer(i):
        return (x + i // NZ) % NX, (z + i % NZ) % NZ

    barrier = pltpu.get_barrier_semaphore()

    def greet(i, carry):
        px, pz = peer(i)
        pl.semaphore_signal(barrier, inc=1, device_id=(px, pz * NY + y, c), device_id_type=MESH)
        return carry

    lax.fori_loop(1, NX * NZ, greet, 0)
    for to in ((x, z * NY + up, c), (x, z * NY + down, c), (x, s, 1 - c)):
        pl.semaphore_signal(barrier, inc=1, device_id=to, device_id_type=MESH)

    for span in range(SPANS):
        vbuf[span, :, :, :, HEAD:] = jnp.ones((NZ, NY * 2, ROWS, HEAD), jnp.bfloat16)

    pl.semaphore_wait(barrier, NX * NZ - 1 + 3)

    def cols(h):
        return pl.ds(pl.multiple_of(h * HEAD, HEAD), HEAD)

    srcs = (k_in, v_in, q_in)

    def block(arr, span, zs, who):
        if arr == Q:
            return qbuf.at[span, zs]
        if arr == K:
            return kbuf.at[span, zs, who]
        return vbuf.at[span, zs, who, :, pl.ds(0, HEAD)]

    whole, low, high = pl.ds(0, NZ), pl.ds(0, NZ // 2), pl.ds(NZ // 2, NZ // 2)
    me = y * 2 + c
    lo, hi, across = down * 2 + c, up * 2 + c, far * 2 + c

    def issue(arr, start=0, stop=NX):
        if start == 0:
            pltpu.make_async_copy(srcs[arr].at[:, cols(head)], block(arr, x, z, me), a2a_recv.at[arr, x]).start()

        def one(i, carry):
            px, pz = peer(i)
            pltpu.make_async_remote_copy(
                src_ref=srcs[arr].at[:, cols(px * NZ + pz)],
                dst_ref=block(arr, x, z, me),
                send_sem=a2a_send.at[arr],
                recv_sem=a2a_recv.at[arr, x],
                device_id=(px, pz * NY + y, c),
                device_id_type=MESH,
            ).start()
            return carry

        lax.fori_loop(max(1, start * NZ), stop * NZ, one, 0)

    def arrived(arr, span):
        b = block(arr, span, whole, me)
        pltpu.make_async_copy(b, b, a2a_recv.at[arr, span]).wait()

    def y_copy(arr, span, zs, who, to, kind):
        b = block(arr, span, zs, who)
        return pltpu.make_async_remote_copy(
            src_ref=b, dst_ref=b, send_sem=y_send.at[arr, span, kind], recv_sem=y_recv.at[arr, span, kind],
            device_id=(x, z * NY + to, c), device_id_type=MESH)

    def c_copy(arr, span, zs, who, kind):
        b = block(arr, span, zs, who)
        return pltpu.make_async_remote_copy(
            src_ref=b, dst_ref=b, send_sem=c_send.at[arr, span, kind], recv_sem=c_recv.at[arr, span, kind],
            device_id=(x, s, 1 - c), device_id_type=MESH)

    def share(arr, span):
        arrived(arr, span)
        y_copy(arr, span, whole, me, up, 0).start()
        y_copy(arr, span, whole, me, down, 1).start()
        c_copy(arr, span, whole, me, 0).start()

    def forward(arr, span):
        y_copy(arr, span, whole, lo, up, 0).wait_recv()
        y_copy(arr, span, low, lo, up, 2).start()
        c_copy(arr, span, whole, lo, 1).start()
        y_copy(arr, span, whole, hi, down, 1).wait_recv()
        y_copy(arr, span, high, hi, down, 3).start()
        c_copy(arr, span, whole, hi, 2).start()

    def finish(arr, span):
        y_copy(arr, span, low, across, up, 2).wait_recv()
        c_copy(arr, span, low, across, 3).start()
        y_copy(arr, span, high, across, down, 3).wait_recv()
        c_copy(arr, span, high, across, 4).start()

    def collect(arr, span):
        for kind, zs in enumerate((whole, whole, whole, low, high)):
            c_copy(arr, span, zs, me, kind).wait_recv()

    def unit(own, span):
        return (own * (own + 1) // 2 + span) * FRAMES

    def score(own, span, masked):
        keys = kbuf[span].reshape(FRAMES * HEAD, HEAD)
        sc = lax.dot_general(
            qbuf[own].reshape(QROWS, HEAD), keys, (((1,), (1,)), ((), ())), preferred_element_type=jnp.float32)
        mx = None if span is own else peak[own]
        for f in range(FRAMES):
            part = sc[:, f * HEAD : (f + 1) * HEAD]
            if masked:
                part = part + jnp.where(mask[own, span * FRAMES + f] > 0, 0.0, NEG).astype(jnp.float32)
            sbuf[unit(own, span) + f] = part
            mx = part if mx is None else jnp.maximum(mx, part)
        peak[own] = mx

    def weigh(own, span, top, total):
        parts = [
            jnp.exp2(sbuf[unit(own, span) + f] * LOG2_SCALE - top).astype(jnp.bfloat16) for f in range(FRAMES)
        ]
        values = vbuf[span].reshape(FRAMES * HEAD, 2 * HEAD)
        return total + jnp.dot(jnp.concatenate(parts, axis=1), values, preferred_element_type=jnp.float32)

    def give(own, dz):
        pz = (z + dz) % NZ
        return pltpu.make_async_remote_copy(
            src_ref=mine.at[own, pz], dst_ref=merged.at[:, cols(head)], send_sem=o_send, recv_sem=o_recv,
            device_id=(own, pz * NY + y, c), device_id_type=MESH)

    def olders(own, start, stop):
        lax.fori_loop(start, stop, lambda i, cur: score(own, i, True) or cur, 0)

    issue(K)
    issue(V)
    issue(Q)

    k0, k1, k2, k3 = [(x + NX - i) % NX for i in range(NX)]
    share(K, k0)
    share(K, k1)
    forward(K, k0)
    share(K, k2)
    forward(K, k1)
    share(K, k3)
    forward(K, k2)
    finish(K, k0)
    forward(K, k3)
    share(V, 0)
    finish(K, k1)
    finish(K, k2)
    share(V, 1)
    finish(K, k3)
    share(V, 2)
    share(V, 3)
    for span in range(SPANS):
        collect(K, span)
    forward(V, 0)

    def outputs(own, last=None):
        top = jnp.broadcast_to(jnp.max(peak[own], axis=1, keepdims=True) * LOG2_SCALE, (QROWS, HEAD))
        total = jnp.zeros((QROWS, 2 * HEAD), jnp.float32)
        if last is None:
            total = lax.fori_loop(0, own + 1, lambda i, cur: weigh(own, i, top, cur), total)
        else:
            total = lax.fori_loop(0, own, lambda i, cur: weigh(own, i, top, cur), total)
            last()
            total = weigh(own, own, top, total)
        result = (total[:, :HEAD] / total[:, HEAD:]).astype(jnp.bfloat16)
        mine[own] = result.reshape(NZ, ROWS, HEAD)
        for dz in range(1, NZ):
            give(own, dz).start()

        @pl.when(x != own)
        def _():
            give(own, 0).start()

        @pl.when(x == own)
        def _():
            pltpu.make_async_copy(mine.at[own, z], merged.at[:, cols(head)], o_recv).start()

    for own in range(SPANS):
        arrived(Q, own)
    score(0, 0, False)
    forward(V, 1)
    score(1, 1, False)
    finish(V, 0)
    forward(V, 2)
    olders(1, 0, 1)
    collect(V, 0)
    outputs(0)
    finish(V, 1)
    forward(V, 3)
    score(2, 2, False)
    collect(V, 1)
    outputs(1)
    olders(2, 0, 1)
    finish(V, 2)
    olders(2, 1, 2)
    score(3, 3, False)
    finish(V, 3)
    collect(V, 2)
    outputs(2)
    olders(3, 0, 3)
    outputs(3, lambda: collect(V, 3))

    pltpu.make_async_copy(merged, merged, o_recv).wait()

    part = merged.at[:, pl.ds(0, FEATURES - HEAD)]
    pltpu.make_async_copy(part, part, o_send).wait()
    for arr in (K, V, Q):
        part = srcs[arr].at[:, pl.ds(0, FEATURES - HEAD)]
        pltpu.make_async_copy(part, part, a2a_send.at[arr]).wait()
    for arr, span in [(arr, span) for arr in (K, V) for span in range(SPANS)]:
        for kind, zs in enumerate((whole, whole, low, high)):
            y_copy(arr, span, zs, me, up, kind).wait_send()
        for kind, zs in enumerate((whole, whole, whole, low, high)):
            c_copy(arr, span, zs, me, kind).wait_send()


def on_device(query_states, key_states, value_states, frame_mask, levels, gate_table):
    bf16 = jnp.bfloat16
    hbm = pl.BlockSpec(memory_space=pl.ANY)
    smem = pl.BlockSpec(memory_space=pltpu.SMEM)
    vmem = pl.BlockSpec(memory_space=pltpu.VMEM)
    dma = pltpu.SemaphoreType.DMA
    result = pl.pallas_call(
        body,
        out_shape=jax.ShapeDtypeStruct((ROWS, FEATURES), bf16),
        in_specs=[smem, hbm, hbm, hbm],
        out_specs=hbm,
        scratch_shapes=[
            pltpu.VMEM((SPANS, NZ, NY * 2, ROWS, HEAD), bf16),
            pltpu.VMEM((SPANS, NZ, NY * 2, ROWS, 2 * HEAD), bf16),
            pltpu.VMEM((SPANS, NZ, ROWS, HEAD), bf16),
            pltpu.VMEM((10 * FRAMES, QROWS, HEAD), jnp.float32),
            pltpu.VMEM((SPANS, QROWS, HEAD), jnp.float32),
            pltpu.VMEM((SPANS, NZ, ROWS, HEAD), bf16),
            dma((3,)),
            dma((3, SPANS)),
            dma((2, SPANS, 4)),
            dma((2, SPANS, 4)),
            dma((2, SPANS, 5)),
            dma((2, SPANS, 5)),
            dma,
            dma,
        ],
        compiler_params=pltpu.CompilerParams(
            collective_id=0, has_side_effects=True, vmem_limit_bytes=63 * 2**20
        ),
    )(frame_mask, query_states[0], key_states[0], value_states[0])
    row = lax.dynamic_slice_in_dim(gate_table, levels[0], 1, axis=0)
    return (row * result.astype(jnp.float32)).astype(bf16)[None]


def solution(mesh):
    split = P("span", ("seq", "tp"), None)
    return jax.shard_map(
        on_device,
        mesh=mesh,
        in_specs=(split, split, split, P(), P("span"), P()),
        out_specs=split,
        check_vma=False,
    )
```

```python
import functools
import math

import jax
import jax.numpy as jnp
from jax import lax
from jax.experimental import pallas as pl
from jax.experimental.pallas import tpu as pltpu
from jax.sharding import PartitionSpec as P

MESH = pl.DeviceIdType.MESH
HEAD = 128
SPANS = 4
NX, NY, NZ = 4, 4, 8
ROWS = 48
FRAMES = 24
QROWS = NZ * ROWS
FEATURES = NX * NZ * HEAD
LOG2_SCALE = math.log2(math.e) / math.sqrt(HEAD)
NEG = -1e30
K, V, Q = 0, 1, 2


def body(
    mask, q_in, k_in, v_in, merged,
    kbuf, vbuf, qbuf, sbuf, peak, mine,
    a2a_send, a2a_recv, y_send, y_recv, c_send, c_recv, o_send, o_recv,
):
    x = lax.axis_index("span")
    s = lax.axis_index("seq")
    c = lax.axis_index("tp")
    y, z = s % NY, s // NY
    up, down, far = (y + 1) % NY, (y + NY - 1) % NY, (y + 2) % NY
    head = x * NZ + z

    def peer(i):
        return (x + i // NZ) % NX, (z + i % NZ) % NZ

    barrier = pltpu.get_barrier_semaphore()

    def greet(i, carry):
        px, pz = peer(i)
        pl.semaphore_signal(barrier, inc=1, device_id=(px, pz * NY + y, c), device_id_type=MESH)
        return carry

    lax.fori_loop(1, NX * NZ, greet, 0)
    for to in ((x, z * NY + up, c), (x, z * NY + down, c), (x, s, 1 - c)):
        pl.semaphore_signal(barrier, inc=1, device_id=to, device_id_type=MESH)

    for span in range(SPANS):
        vbuf[span, :, :, :, HEAD:] = jnp.ones((NZ, NY * 2, ROWS, HEAD), jnp.bfloat16)

    pl.semaphore_wait(barrier, NX * NZ - 1 + 3)

    def cols(h):
        return pl.ds(pl.multiple_of(h * HEAD, HEAD), HEAD)

    srcs = (k_in, v_in, q_in)

    def block(arr, span, zs, who):
        if arr == Q:
            return qbuf.at[span, zs]
        if arr == K:
            return kbuf.at[span, zs, who]
        return vbuf.at[span, zs, who, :, pl.ds(0, HEAD)]

    whole, low, high = pl.ds(0, NZ), pl.ds(0, NZ // 2), pl.ds(NZ // 2, NZ // 2)
    me = y * 2 + c
    lo, hi, across = down * 2 + c, up * 2 + c, far * 2 + c

    def issue(arr, start=0, stop=NX):
        if start == 0:
            pltpu.make_async_copy(srcs[arr].at[:, cols(head)], block(arr, x, z, me), a2a_recv.at[arr, x]).start()

        def one(i, carry):
            px, pz = peer(i)
            pltpu.make_async_remote_copy(
                src_ref=srcs[arr].at[:, cols(px * NZ + pz)],
                dst_ref=block(arr, x, z, me),
                send_sem=a2a_send.at[arr],
                recv_sem=a2a_recv.at[arr, x],
                device_id=(px, pz * NY + y, c),
                device_id_type=MESH,
            ).start()
            return carry

        lax.fori_loop(max(1, start * NZ), stop * NZ, one, 0)

    def arrived(arr, span):
        b = block(arr, span, whole, me)
        pltpu.make_async_copy(b, b, a2a_recv.at[arr, span]).wait()

    def y_copy(arr, span, zs, who, to, kind):
        b = block(arr, span, zs, who)
        return pltpu.make_async_remote_copy(
            src_ref=b, dst_ref=b, send_sem=y_send.at[arr, span, kind], recv_sem=y_recv.at[arr, span, kind],
            device_id=(x, z * NY + to, c), device_id_type=MESH)

    def c_copy(arr, span, zs, who, kind):
        b = block(arr, span, zs, who)
        return pltpu.make_async_remote_copy(
            src_ref=b, dst_ref=b, send_sem=c_send.at[arr, span, kind], recv_sem=c_recv.at[arr, span, kind],
            device_id=(x, s, 1 - c), device_id_type=MESH)

    def share(arr, span):
        arrived(arr, span)
        y_copy(arr, span, whole, me, up, 0).start()
        y_copy(arr, span, whole, me, down, 1).start()
        c_copy(arr, span, whole, me, 0).start()

    def forward(arr, span):
        y_copy(arr, span, whole, lo, up, 0).wait_recv()
        y_copy(arr, span, low, lo, up, 2).start()
        c_copy(arr, span, whole, lo, 1).start()
        y_copy(arr, span, whole, hi, down, 1).wait_recv()
        y_copy(arr, span, high, hi, down, 3).start()
        c_copy(arr, span, whole, hi, 2).start()

    def finish(arr, span):
        y_copy(arr, span, low, across, up, 2).wait_recv()
        c_copy(arr, span, low, across, 3).start()
        y_copy(arr, span, high, across, down, 3).wait_recv()
        c_copy(arr, span, high, across, 4).start()

    def collect(arr, span):
        for kind, zs in enumerate((whole, whole, whole, low, high)):
            c_copy(arr, span, zs, me, kind).wait_recv()

    def unit(own, span):
        return (own * (own + 1) // 2 + span) * FRAMES

    def score(own, span, masked):
        keys = kbuf[span].reshape(FRAMES * HEAD, HEAD)
        sc = lax.dot_general(
            qbuf[own].reshape(QROWS, HEAD), keys, (((1,), (1,)), ((), ())), preferred_element_type=jnp.float32)
        mx = None if span is own else peak[own]
        for f in range(FRAMES):
            part = sc[:, f * HEAD : (f + 1) * HEAD]
            if masked:
                part = part + jnp.where(mask[own, span * FRAMES + f] > 0, 0.0, NEG).astype(jnp.float32)
            sbuf[unit(own, span) + f] = part
            mx = part if mx is None else jnp.maximum(mx, part)
        peak[own] = mx

    def weigh(own, span, top, total):
        parts = [
            jnp.exp2(sbuf[unit(own, span) + f] * LOG2_SCALE - top).astype(jnp.bfloat16) for f in range(FRAMES)
        ]
        values = vbuf[span].reshape(FRAMES * HEAD, 2 * HEAD)
        return total + jnp.dot(jnp.concatenate(parts, axis=1), values, preferred_element_type=jnp.float32)

    def give(own, dz):
        pz = (z + dz) % NZ
        return pltpu.make_async_remote_copy(
            src_ref=mine.at[own, pz], dst_ref=merged.at[:, cols(head)], send_sem=o_send, recv_sem=o_recv,
            device_id=(own, pz * NY + y, c), device_id_type=MESH)

    def olders(own, start, stop):
        lax.fori_loop(start, stop, lambda i, cur: score(own, i, True) or cur, 0)

    issue(K)
    issue(V)
    issue(Q)

    k0, k1, k2, k3 = [(x + NX - i) % NX for i in range(NX)]
    share(K, k0)
    share(K, k1)
    forward(K, k0)
    share(K, k2)
    forward(K, k1)
    share(K, k3)
    forward(K, k2)
    finish(K, k0)
    forward(K, k3)
    share(V, 0)
    finish(K, k1)
    finish(K, k2)
    share(V, 1)
    finish(K, k3)
    share(V, 2)
    share(V, 3)
    for span in range(SPANS):
        collect(K, span)
    forward(V, 0)

    def outputs(own, last=None):
        top = jnp.broadcast_to(jnp.max(peak[own], axis=1, keepdims=True) * LOG2_SCALE, (QROWS, HEAD))
        total = jnp.zeros((QROWS, 2 * HEAD), jnp.float32)
        if last is None:
            total = lax.fori_loop(0, own + 1, lambda i, cur: weigh(own, i, top, cur), total)
        else:
            total = lax.fori_loop(0, own, lambda i, cur: weigh(own, i, top, cur), total)
            last()
            total = weigh(own, own, top, total)
        result = (total[:, :HEAD] / total[:, HEAD:]).astype(jnp.bfloat16)
        mine[own] = result.reshape(NZ, ROWS, HEAD)
        for dz in range(1, NZ):
            give(own, dz).start()

        @pl.when(x != own)
        def _():
            give(own, 0).start()

        @pl.when(x == own)
        def _():
            pltpu.make_async_copy(mine.at[own, z], merged.at[:, cols(head)], o_recv).start()

    for own in range(SPANS):
        arrived(Q, own)
    score(0, 0, False)
    forward(V, 1)
    score(1, 1, False)
    finish(V, 0)
    forward(V, 2)
    olders(1, 0, 1)
    collect(V, 0)
    outputs(0)
    finish(V, 1)
    forward(V, 3)
    score(2, 2, False)
    collect(V, 1)
    outputs(1)
    olders(2, 0, 1)
    finish(V, 2)
    olders(2, 1, 2)
    score(3, 3, False)
    finish(V, 3)
    olders(3, 0, 3)
    collect(V, 2)
    outputs(2)
    outputs(3, lambda: collect(V, 3))

    pltpu.make_async_copy(merged, merged, o_recv).wait()

    part = merged.at[:, pl.ds(0, FEATURES - HEAD)]
    pltpu.make_async_copy(part, part, o_send).wait()
    for arr in (K, V, Q):
        part = srcs[arr].at[:, pl.ds(0, FEATURES - HEAD)]
        pltpu.make_async_copy(part, part, a2a_send.at[arr]).wait()
    for arr, span in [(arr, span) for arr in (K, V) for span in range(SPANS)]:
        for kind, zs in enumerate((whole, whole, low, high)):
            y_copy(arr, span, zs, me, up, kind).wait_send()
        for kind, zs in enumerate((whole, whole, whole, low, high)):
            c_copy(arr, span, zs, me, kind).wait_send()


def on_device(query_states, key_states, value_states, frame_mask, levels, gate_table):
    bf16 = jnp.bfloat16
    hbm = pl.BlockSpec(memory_space=pl.ANY)
    smem = pl.BlockSpec(memory_space=pltpu.SMEM)
    vmem = pl.BlockSpec(memory_space=pltpu.VMEM)
    dma = pltpu.SemaphoreType.DMA
    result = pl.pallas_call(
        body,
        out_shape=jax.ShapeDtypeStruct((ROWS, FEATURES), bf16),
        in_specs=[smem, hbm, hbm, hbm],
        out_specs=hbm,
        scratch_shapes=[
            pltpu.VMEM((SPANS, NZ, NY * 2, ROWS, HEAD), bf16),
            pltpu.VMEM((SPANS, NZ, NY * 2, ROWS, 2 * HEAD), bf16),
            pltpu.VMEM((SPANS, NZ, ROWS, HEAD), bf16),
            pltpu.VMEM((10 * FRAMES, QROWS, HEAD), jnp.float32),
            pltpu.VMEM((SPANS, QROWS, HEAD), jnp.float32),
            pltpu.VMEM((SPANS, NZ, ROWS, HEAD), bf16),
            dma((3,)),
            dma((3, SPANS)),
            dma((2, SPANS, 4)),
            dma((2, SPANS, 4)),
            dma((2, SPANS, 5)),
            dma((2, SPANS, 5)),
            dma,
            dma,
        ],
        compiler_params=pltpu.CompilerParams(
            collective_id=0, has_side_effects=True, vmem_limit_bytes=63 * 2**20
        ),
    )(frame_mask, query_states[0], key_states[0], value_states[0])
    row = lax.dynamic_slice_in_dim(gate_table, levels[0], 1, axis=0)
    return (row * result.astype(jnp.float32)).astype(bf16)[None]


def solution(mesh):
    split = P("span", ("seq", "tp"), None)
    return jax.shard_map(
        on_device,
        mesh=mesh,
        in_specs=(split, split, split, P(), P("span"), P()),
        out_specs=split,
        check_vma=False,
    )
```
